256 devices in a mesh: req: 4 (over x), seq: 32 (over z, y), tp: 2 (over core).
Axes of the slice: x: 4, y: 4, z: 8, core: 2. Of those that a mesh axis runs over, the one named last changes fastest.
Arguments:
- keys: bfloat16 [4, 32768, 4, 8, 128], P('req', 'seq', None, 'tp'), may hold values from -40 to 40
- start_basis: bfloat16 [4, 4, 8, 128, 256], P('req', None, 'tp'), may hold values from -0.09375 to 0.09375
- owner_map: int32 [4, 32, 16], P('req', 'seq'), may hold values from 0 to 15, each once within a row
Outputs:
- handed: bfloat16 [4, 32, 4, 256, 256], P('req', 'seq')
The draws below stay inside these ranges and needn't reach their ends.
Inputs may be any that keep to these rules, and one draw needn't show every extreme that they name: Each row owner_map[r, s, :] is a permutation of 0 to 15: block b goes to decode owner owner_map[r, s, b] // 4, slot owner_map[r, s, b] % 4.
All inputs are finite; a program needn't handle non-finite values.
Results may differ from the reference program's by a relative error of at most 0.0085.
Values may be sent and summed in bfloat16 or wider, within the bound.
A program may use at most 64 MiB of HBM per device.

```python
import jax
import jax.numpy as jnp
from jax import lax

LAYERS = 4
KVH = 8
HD = 128
RANK = 256
ITERS = 2
BLK = 64
KW = 4096
REQS = 4
SHARDS = 32
SEQLEN = 32768
NBLK = 16
PER = 4


def draw_keys(key, part):
    key = jax.random.fold_in(key, 7)
    channel_key, token_key, noise_key = jax.random.split(key, 3)
    channel_scale = jnp.exp(jax.random.uniform(channel_key, (1, 1, LAYERS, KVH, HD), jnp.float32, -0.7, 0.7))
    position = jnp.arange(SEQLEN, dtype=jnp.float32) / SEQLEN
    position_gain = (1.0 + 2.0 * position).reshape(1, SEQLEN, 1, 1, 1)
    token_scale = jnp.exp(jax.random.uniform(token_key, (REQS, SEQLEN, 1, 1, 1), jnp.float32, -1.15, 1.15))
    noise_part = jax.random.truncated_normal(noise_key, -4.0, 4.0, (REQS, SEQLEN, LAYERS, KVH, HD), jnp.float32)
    return (0.3 * noise_part * channel_scale * token_scale * position_gain).astype(jnp.bfloat16)


def levels(rng, extent, cuts, smallest, largest):
    factor_of, own = 1.0, jax.random.fold_in(rng, 6)
    for dim, parts in cuts:
        steps = jnp.exp(jax.random.uniform(jax.random.fold_in(own, dim), (parts,), jnp.float32, smallest / len(cuts), largest / len(cuts)))
        factor_of = factor_of * jnp.repeat(steps, extent[dim] // parts).reshape([-1 if axis == dim else 1 for axis in range(len(extent))])
    return factor_of


def noise(rng, extent, scale, most, pieces=(), kind=jnp.bfloat16):
    result = jax.random.normal(rng, extent, jnp.float32) * scale
    if len(pieces) > 0:
        result = levels(rng, extent, pieces, -0.22, 0.18) * result
    return jnp.clip(result, min=-most, max=most).astype(kind)


def setup_inputs(seed: int = 0) -> dict:
    streams_of = jax.random.split(jax.random.key(seed), 4)
    keys = draw_keys(jax.random.fold_in(streams_of[3], 71), 0)
    start_basis = noise(streams_of[1], (REQS, LAYERS, KVH, HD, RANK), KW ** -0.5, 0.09375, ((0, 4), (2, 2)))
    owner_map = jax.vmap(lambda own: jax.random.permutation(own, NBLK))(jax.random.split(streams_of[2], REQS * SHARDS)).reshape((REQS, SHARDS, NBLK)).astype(jnp.int32)
    return {"keys": keys, "start_basis": start_basis, "owner_map": owner_map}


def orthonormalize(moment):
    gram_matrix = jnp.dot(moment.T.astype(jnp.float32), moment.astype(jnp.float32), precision=lax.Precision.HIGHEST, preferred_element_type=jnp.float32)
    shift_value = 0.0001 * jnp.trace(gram_matrix) / RANK
    gram_matrix = gram_matrix + shift_value * jnp.eye(RANK, dtype=jnp.float32)
    factor = jnp.linalg.cholesky(gram_matrix)
    return jax.scipy.linalg.solve_triangular(factor, moment.T, lower=True).T

def coefficients_of(key_rows, first_basis):
    basis_now = first_basis
    for iteration in range(ITERS):
        projected = jnp.dot(key_rows.astype(jnp.float32), basis_now.astype(jnp.float32), preferred_element_type=jnp.float32).astype(jnp.bfloat16)
        moment = jnp.dot(key_rows.T.astype(jnp.float32), projected.astype(jnp.float32), preferred_element_type=jnp.float32)
        basis_now = orthonormalize(moment).astype(jnp.bfloat16)
    return jnp.dot(key_rows.astype(jnp.float32), basis_now.astype(jnp.float32), preferred_element_type=jnp.float32).astype(jnp.bfloat16)

def reference(keys, start_basis, owner_map):
    results = []
    for request in range(REQS):
        key_rows = keys[request].reshape(SEQLEN, KW)
        results.append(coefficients_of(key_rows, start_basis[request].reshape(KW, RANK)))
    coefficients = jnp.stack(results)
    blocks = coefficients.reshape(REQS, SHARDS, NBLK, BLK, RANK)
    inverse = jnp.argsort(owner_map, axis=-1).astype(jnp.int32)
    placed = jnp.take_along_axis(blocks, inverse[:, :, :, None, None], axis=2)
    placed = placed.reshape(REQS, SHARDS, REQS, PER * BLK, RANK)
    return jnp.transpose(placed, (2, 1, 0, 3, 4))
```

```python
import functools

import jax
import jax.numpy as jnp
from jax import lax
from jax.experimental import pallas as pl
from jax.experimental.pallas import tpu as pltpu
from jax.sharding import PartitionSpec as P

MESH = pl.DeviceIdType.MESH
HI = lax.Precision.HIGHEST
F32 = jnp.float32
B16 = jnp.bfloat16
YS, ZS = 4, 8
TILE = 256


def dot_nt(a, b, precision=None):
    return lax.dot_general(
        a, b, (((1,), (1,)), ((), ())), precision=precision, preferred_element_type=F32
    )


def dot_tn(a, b, precision=None):
    return lax.dot_general(
        a, b, (((0,), (0,)), ((), ())), precision=precision, preferred_element_type=F32
    )


def eliminate(block):
    b = block.shape[0]
    low = block
    done = []
    for p in range(b // 8):
        height = low.shape[0]
        row = lax.broadcasted_iota(jnp.int32, (height, 128), 0)
        cols = [
            jnp.broadcast_to(low[:, 8 * p + j : 8 * p + j + 1], (height, 128)) for j in range(8)
        ]
        diag = jnp.ones((8, 128), F32)
        for j in range(8):
            pivot = jnp.broadcast_to(cols[j][j : j + 1, :], (8, 128))
            guess = pl.reciprocal(pivot, approx=True)
            inverse = guess * (2.0 - pivot * guess)
            diag = jnp.where(row[:8] == j, pivot, diag)
            factor = cols[j] * jnp.broadcast_to(inverse[:1], (height, 128))
            factor = jnp.where(row > j, factor, 0.0)
            low = low - factor * jnp.broadcast_to(low[j : j + 1, :], (height, 128))
            for m in range(j + 1, 8):
                cols[m] = cols[m] - factor * jnp.broadcast_to(
                    cols[m][j : j + 1, :], (height, 128)
                )
        done.append(low[:8] * lax.rsqrt(diag))
        low = low[8:]
    return jnp.concatenate(done, axis=0)[:, b:]


def invert_factor(gram, out, state):
    n = gram.shape[0]
    b = 64
    r = lax.broadcasted_iota(jnp.int32, (n, n), 0)
    c = lax.broadcasted_iota(jnp.int32, (n, n), 1)
    shift = 0.0001 * jnp.sum(jnp.where(r == c, gram, 0.0)) / n
    state[...] = jnp.where(r == c, gram + shift, gram)
    eye = jnp.where(r[:b, :b] == c[:b, :b], 1.0, 0.0).astype(F32)
    for step in range(n // b):
        lo, hi = step * b, (step + 1) * b
        band = state[lo:hi, :]
        inverse = eliminate(jnp.concatenate([band[:, lo:hi], eye], axis=1))
        parts = ([band[:, :lo]] if lo else []) + [eye] + ([band[:, hi:]] if hi < n else [])
        x = jnp.dot(
            inverse, jnp.concatenate(parts, axis=1), precision=HI, preferred_element_type=F32
        )
        out[lo:hi, :] = jnp.where(c[lo:hi, :] < hi, x, 0.0)
        if hi < n:
            rest = state[hi:, :]
            lane = c[hi:, :]
            rest = jnp.where((lane >= lo) & (lane < hi), 0.0, rest)
            state[hi:, :] = rest - dot_tn(x[:, hi:], x, precision=HI)


def factor_kernel(g_ref, out_ref, state):
    invert_factor(g_ref[...], out_ref, state)


def factor_call(gram):
    n = gram.shape[0]
    return pl.pallas_call(
        factor_kernel,
        out_shape=jax.ShapeDtypeStruct((n, n), F32),
        scratch_shapes=[pltpu.VMEM((n, n), F32)],
        name="factor",
    )(gram)


class Links:
    def __init__(self, send, recv):
        self.send, self.recv, self.count = send, recv, 0

    def copy(self, src, dst, **device):
        i = self.count
        self.count += 1
        return pltpu.make_async_remote_copy(
            src_ref=src,
            dst_ref=dst,
            send_sem=self.send.at[i],
            recv_sem=self.recv.at[i],
            device_id=device,
            device_id_type=MESH,
        )


def greet(partners):
    barrier = pltpu.get_barrier_semaphore()
    for device in partners:
        pl.semaphore_signal(barrier, inc=1, device_id=device, device_id_type=MESH)
    pl.semaphore_wait(barrier, len(partners))


def moment_kernel(first, *refs):
    if first:
        k, basis = refs[:2]
    else:
        k, pin, winv = refs[:3]
    refs = refs[2 if first else 3 :]
    (
        pout, gout, p_own, p_in, z_in, zt, opp, in_a, in_b, right32, left32, right16, left16,
        from_left, from_right, own, zsend, zin, full, g_own, g_in, send, recv,
    ) = refs
    s = lax.axis_index("seq")
    c = lax.axis_index("tp")
    y, z = s % YS, s // YS
    links = Links(send, recv)

    def at_y(d):
        return z * YS + (y + d) % YS

    def at_z(d):
        return ((z + d) % ZS) * YS + y

    greet(
        [{"tp": 1 - c}]
        + [{"seq": at_y(d)} for d in range(1, YS)]
        + [{"seq": at_z(d)} for d in range(1, ZS)]
    )
    tokens = k.shape[0]
    tiles = tokens // TILE

    if first:
        swaps = []
        for i in range(tiles):
            rows = pl.ds(i * TILE, TILE)
            p_own[rows, :] = jnp.dot(k[rows, :], basis[...], preferred_element_type=F32)
            copy = links.copy(p_own.at[rows], z_in.at[rows], tp=1 - c)
            copy.start()
            swaps.append(copy)
        for i in range(tiles):
            rows = pl.ds(i * TILE, TILE)
            swaps[i].wait_recv()
            zt[:, rows] = (p_own[rows, :] + z_in[rows, :]).T.astype(B16)
        for copy in swaps:
            copy.wait_send()
    else:
        for i in range(tiles):
            rows = pl.ds(i * TILE, TILE)
            zt[:, rows] = dot_nt(winv[...], pin[rows, :], precision=HI).astype(B16)

    def quarter(q):
        groups = []
        for t in range(2):
            cols = pl.ds(pl.multiple_of(q * 512 + t * 256, 256), 256)
            product = jnp.dot(zt[...], k[:, cols], preferred_element_type=F32)
            groups += [product[:, :128], product[:, 128:]]
        return groups

    a, b = pl.ds(0, 2), pl.ds(2, 2)
    right, left = at_y(1), at_y(3)
    for g, value in enumerate(quarter((y + 2) % YS)):
        opp[g] = value.astype(B16)
    r1 = links.copy(opp.at[a], in_a, seq=right)
    l1 = links.copy(opp.at[b], in_b, seq=left)
    r1.start()
    l1.start()
    for g, value in enumerate(quarter((y + 1) % YS)):
        if g < 2:
            right32[g] = value
        else:
            right16[g] = value.astype(B16)
    r2b = links.copy(right16.at[b], from_left.at[b], seq=right)
    r2b.start()
    for g, value in enumerate(quarter((y + 3) % YS)):
        if g < 2:
            left16[g] = value.astype(B16)
        else:
            left32[g - 2] = value
    l2a = links.copy(left16.at[a], from_right.at[a], seq=left)
    l2a.start()
    for g, value in enumerate(quarter(y)):
        own[g] = value
    r1.wait_recv()
    right16[a] = (right32[...] + in_a[...].astype(F32)).astype(B16)
    r2a = links.copy(right16.at[a], from_left.at[a], seq=right)
    r2a.start()
    l1.wait_recv()
    left16[b] = (left32[...] + in_b[...].astype(F32)).astype(B16)
    l2b = links.copy(left16.at[b], from_right.at[b], seq=left)
    l2b.start()
    r2b.wait_recv()
    l2b.wait_recv()
    own[b] = own[b] + from_left[b].astype(F32) + from_right[b].astype(F32)
    r2a.wait_recv()
    l2a.wait_recv()
    own[a] = own[a] + from_left[a].astype(F32) + from_right[a].astype(F32)

    for piece in range(ZS):
        zsend[piece] = own[piece // 2, 128 * (piece % 2) : 128 * (piece % 2) + 128, :].astype(B16)
    scatter = []
    for d in (4, 3, 5, 2, 6, 1, 7):
        copy = links.copy(zsend.at[(z + d) % ZS], zin.at[d - 1], seq=at_z(d))
        copy.start()
        scatter.append(copy)
    total = own[z // 2, pl.ds(pl.multiple_of((z % 2) * 128, 128), 128), :]
    for copy in scatter:
        copy.wait_recv()
    for d in range(1, ZS):
        total = total + zin[d - 1].astype(F32)
    full[y, z] = total.astype(B16)
    gather = []
    for d in (4, 3, 5, 2, 6, 1, 7):
        copy = links.copy(full.at[y, z], full.at[y, z], seq=at_z(d))
        copy.start()
        gather.append(copy)
    for copy in [r1, l1, r2b, l2a, r2a, l2b] + scatter:
        copy.wait_send()
    for copy in gather:
        copy.wait_recv()

    a, b = pl.ds(0, 4), pl.ds(4, 4)
    yl, yr, yo = (y + 3) % YS, (y + 1) % YS, (y + 2) % YS

    def pass_on(q, half, to):
        copy = links.copy(full.at[q, half], full.at[q, half], seq=to)
        copy.start()
        return copy

    ra, lb = pass_on(y, a, right), pass_on(y, b, left)
    rb, la = pass_on(y, b, right), pass_on(y, a, left)

    def absorb(q, start):
        groups = [
            jnp.concatenate([full[q, 2 * g], full[q, 2 * g + 1]], axis=0) for g in range(4)
        ]
        block = jnp.concatenate(groups, axis=1)
        cols = pl.ds(pl.multiple_of(q * 512, 512), 512)
        product = dot_nt(block, block)
        g_own[...] = product if start else g_own[...] + product
        for i in range(tiles):
            rows = pl.ds(i * TILE, TILE)
            product = dot_nt(k[rows, cols], block)
            p_own[rows, :] = product if start else p_own[rows, :] + product

    absorb(y, True)
    ra.wait_recv()
    fa = pass_on(yl, a, right)
    lb.wait_recv()
    fb = pass_on(yr, b, left)
    rb.wait_recv()
    absorb(yl, False)
    la.wait_recv()
    absorb(yr, False)
    fa.wait_recv()
    fb.wait_recv()
    absorb(yo, False)

    swap = links.copy(g_own, g_in, tp=1 - c)
    swap.start()
    swaps = []
    for i in range(tiles):
        rows = pl.ds(i * TILE, TILE)
        copy = links.copy(p_own.at[rows], p_in.at[rows], tp=1 - c)
        copy.start()
        swaps.append(copy)
    swap.wait_recv()
    gout[...] = g_own[...] + g_in[...]
    for i in range(tiles):
        rows = pl.ds(i * TILE, TILE)
        swaps[i].wait_recv()
        pout[rows, :] = p_own[rows, :] + p_in[rows, :]
    for copy in gather + [ra, rb, la, lb, fa, fb, swap] + swaps:
        copy.wait_send()


def moment_call(first, keys, *args):
    tokens = keys.shape[0]
    vm = pltpu.VMEM
    return pl.pallas_call(
        functools.partial(moment_kernel, first),
        out_shape=(
            jax.ShapeDtypeStruct((tokens, 256), F32),
            jax.ShapeDtypeStruct((256, 256), F32),
        ),
        in_specs=[pl.BlockSpec(memory_space=vm)] * (1 + len(args)),
        out_specs=(pl.BlockSpec(memory_space=vm),) * 2,
        scratch_shapes=[
            vm((tokens, 256), F32),
            vm((tokens, 256), F32),
            vm((tokens if first else 8, 256), F32),
            vm((256, tokens), B16),
            vm((4, 256, 128), B16),
            vm((2, 256, 128), B16),
            vm((2, 256, 128), B16),
            vm((2, 256, 128), F32),
            vm((2, 256, 128), F32),
            vm((4, 256, 128), B16),
            vm((4, 256, 128), B16),
            vm((4, 256, 128), B16),
            vm((4, 256, 128), B16),
            vm((4, 256, 128), F32),
            vm((8, 128, 128), B16),
            vm((7, 128, 128), B16),
            vm((4, 8, 128, 128), B16),
            vm((256, 256), F32),
            vm((256, 256), F32),
            pltpu.SemaphoreType.DMA((40,)),
            pltpu.SemaphoreType.DMA((40,)),
        ],
        compiler_params=pltpu.CompilerParams(
            collective_id=0 if first else 1,
            has_side_effects=True,
            vmem_limit_bytes=40 * 2**20,
        ),
        name="moment_first" if first else "moment_next",
    )(keys, *args)


def hand_kernel(order, p, winv, out, coef, outbox, halves, send, recv):
    x = lax.axis_index("req")
    c = lax.axis_index("tp")
    links = Links(send, recv)
    greet([{"tp": 1 - c}] + [{"req": (x + d) % 4} for d in range(1, 4)])
    tokens = p.shape[0]
    half = winv[pl.ds(pl.multiple_of(c * 128, 128), 128), :]
    for i in range(tokens // TILE):
        rows = pl.ds(i * TILE, TILE)
        rounded = dot_nt(p[rows, :], half, precision=HI).astype(B16)
        for b in range(TILE // 64):
            coef[i * (TILE // 64) + b] = rounded[64 * b : 64 * b + 64, :]
    for slot in range(16):
        outbox[slot // 4, 64 * (slot % 4) : 64 * (slot % 4) + 64, :] = coef[order[slot]]
    away = []
    for d in (2, 1, 3):
        o = (x + d) % 4
        copy = links.copy(outbox.at[o], halves.at[c, x], req=o)
        copy.start()
        away.append((d, copy))
    halves[c, x] = outbox[x]
    across = []

    def cross(r):
        copy = links.copy(halves.at[c, r], halves.at[c, r], tp=1 - c)
        copy.start()
        across.append(copy)

    cross(x)
    for d, copy in away:
        copy.wait_recv()
        cross((x + 4 - d) % 4)
    for copy in across:
        copy.wait_recv()
    for r in range(4):
        out[r, :, :128] = halves[0, r]
        out[r, :, 128:] = halves[1, r]
    for _, copy in away:
        copy.wait_send()
    for copy in across:
        copy.wait_send()


def hand_call(order, p, winv):
    tokens = p.shape[0]
    vm = pltpu.VMEM
    return pl.pallas_call(
        hand_kernel,
        out_shape=jax.ShapeDtypeStruct((4, 256, 256), B16),
        in_specs=[pl.BlockSpec(memory_space=pltpu.SMEM)] + [pl.BlockSpec(memory_space=vm)] * 2,
        out_specs=pl.BlockSpec(memory_space=vm),
        scratch_shapes=[
            vm((16, 64, 128), B16),
            vm((4, 256, 128), B16),
            vm((2, 4, 256, 128), B16),
            pltpu.SemaphoreType.DMA((8,)),
            pltpu.SemaphoreType.DMA((8,)),
        ],
        compiler_params=pltpu.CompilerParams(
            collective_id=2, has_side_effects=True, vmem_limit_bytes=16 * 2**20
        ),
        name="hand",
    )(order, p, winv)


def body(keys, start_basis, owner_map):
    tokens = keys.shape[1]
    key_rows = keys.reshape(tokens, -1)
    basis = start_basis.reshape(key_rows.shape[1], -1)
    owners = owner_map.reshape(-1)
    slots = jnp.arange(owners.shape[0], dtype=jnp.int32)
    order = jnp.sum(jnp.where(owners[None, :] == slots[:, None], slots[None, :], 0), axis=1)
    p, gram = moment_call(True, key_rows, basis)
    winv = factor_call(gram)
    p, gram = moment_call(False, key_rows, p, winv)
    winv = factor_call(gram)
    handed = hand_call(order, p, winv)
    return handed[None, None]


def solution(mesh):
    placed = (
        P("req", "seq", None, "tp", None),
        P("req", None, "tp", None, None),
        P("req", "seq", None),
    )
    return jax.shard_map(
        body,
        mesh=mesh,
        in_specs=placed,
        out_specs=P("req", "seq", None, None, None),
        check_vma=False,
    )
```

```python
import jax
import jax.numpy as jnp
from jax import lax
from jax.experimental import pallas as pl
from jax.experimental.pallas import tpu as pltpu
from jax.sharding import PartitionSpec as P

MESH = pl.DeviceIdType.MESH
HI = lax.Precision.HIGHEST
F32 = jnp.float32
B16 = jnp.bfloat16
YS, ZS = 4, 8
ITERS = 2
TILE = 256
FEATS = 128
CHUNKS = 4
PIECE = 256 // ZS


def dot_nt(a, b, precision=None):
    return lax.dot_general(
        a, b, (((1,), (1,)), ((), ())), precision=precision, preferred_element_type=F32
    )


def dot_tn(a, b, precision=None):
    return lax.dot_general(
        a, b, (((0,), (0,)), ((), ())), precision=precision, preferred_element_type=F32
    )


def eliminate(block):
    b = block.shape[0]
    low = block
    done = []
    for p in range(b // 8):
        height = low.shape[0]
        row = lax.broadcasted_iota(jnp.int32, (height, 128), 0)
        cols = [
            jnp.broadcast_to(low[:, 8 * p + j : 8 * p + j + 1], (height, 128)) for j in range(8)
        ]
        diag = jnp.ones((8, 128), F32)
        for j in range(8):
            pivot = jnp.broadcast_to(cols[j][j : j + 1, :], (8, 128))
            guess = pl.reciprocal(pivot, approx=True)
            inverse = guess * (2.0 - pivot * guess)
            diag = jnp.where(row[:8] == j, pivot, diag)
            factor = cols[j] * jnp.broadcast_to(inverse[:1], (height, 128))
            factor = jnp.where(row > j, factor, 0.0)
            low = low - factor * jnp.broadcast_to(low[j : j + 1, :], (height, 128))
            for m in range(j + 1, 8):
                cols[m] = cols[m] - factor * jnp.broadcast_to(
                    cols[m][j : j + 1, :], (height, 128)
                )
        done.append(low[:8] * lax.rsqrt(diag))
        low = low[8:]
    return jnp.concatenate(done, axis=0)[:, b:]


def invert_factor(gram, out, state):
    n = gram.shape[0]
    b = 64
    r = lax.broadcasted_iota(jnp.int32, (n, n), 0)
    c = lax.broadcasted_iota(jnp.int32, (n, n), 1)
    shift = 0.0001 * jnp.sum(jnp.where(r == c, gram, 0.0)) / n
    state[...] = jnp.where(r == c, gram + shift, gram)
    eye = jnp.where(r[:b, :b] == c[:b, :b], 1.0, 0.0).astype(F32)
    for step in range(n // b):
        lo, hi = step * b, (step + 1) * b
        band = state[lo:hi, :]
        inverse = eliminate(jnp.concatenate([band[:, lo:hi], eye], axis=1))
        parts = ([band[:, :lo]] if lo else []) + [eye] + ([band[:, hi:]] if hi < n else [])
        x = jnp.dot(
            inverse, jnp.concatenate(parts, axis=1), precision=HI, preferred_element_type=F32
        )
        out[lo:hi, :] = jnp.where(c[lo:hi, :] < hi, x, 0.0)
        if hi < n:
            rest = state[hi:, :]
            lane = c[hi:, :]
            rest = jnp.where((lane >= lo) & (lane < hi), 0.0, rest)
            state[hi:, :] = rest - dot_tn(x[:, hi:], x, precision=HI)


class Links:
    def __init__(self, send, recv):
        self.send, self.recv, self.count, self.open = send, recv, 0, []

    def start(self, src, dst, **device):
        i = self.count
        self.count += 1
        copy = pltpu.make_async_remote_copy(
            src_ref=src,
            dst_ref=dst,
            send_sem=self.send.at[i],
            recv_sem=self.recv.at[i],
            device_id=device,
            device_id_type=MESH,
        )
        copy.start()
        self.open.append(copy)
        return copy

    def drain(self):
        for copy in self.open:
            copy.wait_send()
        self.open = []


def greet(partners):
    barrier = pltpu.get_barrier_semaphore()
    for device in partners:
        pl.semaphore_signal(barrier, inc=1, device_id=device, device_id_type=MESH)
    pl.semaphore_wait(barrier, len(partners))


COPIES = 4 + ITERS * (CHUNKS * (6 + 14 + 6) + 1 + 4) + 7


def subspace_kernel(
    order, keys, basis, out,
    raw, k, v0, zt, p_own, z_in, p_in, opp, right32, left32, right16, left16, own, zsend,
    in_a, in_b, from_left, from_right, zin, full, g_own, g_in, state, winv,
    coef, outbox, halves, load, send, recv,
):
    x = lax.axis_index("req")
    s = lax.axis_index("seq")
    c = lax.axis_index("tp")
    y, z = s % YS, s // YS
    links = Links(send, recv)
    tokens = k.shape[0]
    tiles = tokens // TILE

    def at_y(d):
        return z * YS + (y + d) % YS

    def at_z(d):
        return ((z + d) % ZS) * YS + y

    right, left = at_y(1), at_y(3)
    yr, yo, yl = (y + 1) % YS, (y + 2) % YS, (y + 3) % YS
    far_first = (4, 3, 5, 2, 6, 1, 7)
    top, low = pl.ds(0, 128), pl.ds(128, 128)

    def tile(i):
        return pl.ds(i * TILE, TILE)

    loads = [pltpu.make_async_copy(basis, v0, load.at[tiles])]
    for i in range(tiles):
        loads.append(pltpu.make_async_copy(keys.at[0, tile(i)], raw.at[tile(i)], load.at[i]))
    for copy in loads:
        copy.start()
    greet(
        [{"tp": 1 - c}]
        + [{"seq": at_y(d)} for d in range(1, YS)]
        + [{"seq": at_z(d)} for d in range(1, ZS)]
        + [{"req": (x + d) % 4} for d in range(1, 4)]
    )

    loads[0].wait()
    swaps = []
    for i in range(tiles):
        loads[1 + i].wait()
        k[tile(i), :] = raw[tile(i)].reshape(TILE, k.shape[1])
        p_own[tile(i), :] = jnp.dot(k[tile(i), :], v0[...], preferred_element_type=F32)
        swaps.append(links.start(p_own.at[tile(i)], z_in.at[tile(i)], tp=1 - c))
    for i in range(tiles):
        swaps[i].wait_recv()
        zt[:, tile(i)] = (p_own[tile(i), :] + z_in[tile(i), :]).T.astype(B16)
    links.drain()

    for it in range(ITERS):
        run = {}

        def moment(q, j):
            cols = pl.ds(pl.multiple_of(q * (CHUNKS * FEATS) + j * FEATS, FEATS), FEATS)
            return jnp.dot(zt[...], k[:, cols], preferred_element_type=F32)

        def stage0(j):
            opp[j] = moment(yo, j).astype(B16)
            run["r1", j] = links.start(opp.at[j, top], in_a.at[it, j], seq=right)
            run["l1", j] = links.start(opp.at[j, low], in_b.at[it, j], seq=left)
            value = moment(yr, j)
            right32[j] = value[:128]
            right16[j, 128:, :] = value[128:].astype(B16)
            run["r2b", j] = links.start(
                right16.at[j, low], from_left.at[it, j, low], seq=right
            )
            value = moment(yl, j)
            left32[j] = value[128:]
            left16[j, :128, :] = value[:128].astype(B16)
            run["l2a", j] = links.start(left16.at[j, top], from_right.at[it, j, top], seq=left)
            own[j] = moment(y, j)

        def stage1(j):
            run["r1", j].wait_recv()
            right16[j, :128, :] = (right32[j] + in_a[it, j].astype(F32)).astype(B16)
            run["r2a", j] = links.start(
                right16.at[j, top], from_left.at[it, j, top], seq=right
            )
            run["l1", j].wait_recv()
            left16[j, 128:, :] = (left32[j] + in_b[it, j].astype(F32)).astype(B16)
            run["l2b", j] = links.start(left16.at[j, low], from_right.at[it, j, low], seq=left)

        def stage2(j):
            for name in ("r2b", "l2a", "r2a", "l2b"):
                run[name, j].wait_recv()
            value = own[j] + from_left[it, j].astype(F32) + from_right[it, j].astype(F32)
            own[j] = value
            zsend[j] = value.astype(B16)
            for d in far_first:
                rows = pl.ds(pl.multiple_of((z + d) % ZS * PIECE, PIECE), PIECE)
                run["zs", d, j] = links.start(
                    zsend.at[j, rows], zin.at[it, j, d - 1], seq=at_z(d)
                )

        def stage3(j):
            mine = pl.ds(pl.multiple_of(z * PIECE, PIECE), PIECE)
            total = own[j, mine, :]
            for d in far_first:
                run["zs", d, j].wait_recv()
            for d in range(1, ZS):
                total = total + zin[it, j, d - 1].astype(F32)
            full[it, y, j, mine, :] = total.astype(B16)
            for d in far_first:
                run["zg", d, j] = links.start(
                    full.at[it, y, j, mine], full.at[it, y, j, mine], seq=at_z(d)
                )

        def pass_on(q, j, half, to):
            return links.start(full.at[it, q, j, half], full.at[it, q, j, half], seq=to)

        def absorb(q, j, start=False):
            block = full[it, q, j]
            cols = pl.ds(pl.multiple_of(q * (CHUNKS * FEATS) + j * FEATS, FEATS), FEATS)
            product = dot_nt(block, block)
            g_own[...] = product if start else g_own[...] + product
            for i in range(tiles):
                product = dot_nt(k[tile(i), cols], block)
                p_own[tile(i), :] = product if start else p_own[tile(i), :] + product

        def stage4(j):
            for d in far_first:
                run["zg", d, j].wait_recv()
            run["ra", j] = pass_on(y, j, top, right)
            run["lb", j] = pass_on(y, j, low, left)
            run["rb", j] = pass_on(y, j, low, right)
            run["la", j] = pass_on(y, j, top, left)
            absorb(y, j, start=j == 0)

        def stage5(j):
            run["ra", j].wait_recv()
            run["fa", j] = pass_on(yl, j, top, right)
            run["lb", j].wait_recv()
            run["fb", j] = pass_on(yr, j, low, left)

        def stage6(j):
            run["rb", j].wait_recv()
            absorb(yl, j)
            run["la", j].wait_recv()
            absorb(yr, j)

        def stage7(j):
            run["fa", j].wait_recv()
            run["fb", j].wait_recv()
            absorb(yo, j)

        stages = (stage0, stage1, stage2, stage3, stage4, stage5, stage6, stage7)
        for step in range(CHUNKS + len(stages) - 1):
            for at, stage in enumerate(stages):
                if 0 <= step - at < CHUNKS:
                    stage(step - at)

        swap = links.start(g_own, g_in.at[it], tp=1 - c)
        swaps = [
            links.start(p_own.at[tile(i)], p_in.at[it, tile(i)], tp=1 - c) for i in range(tiles)
        ]
        swap.wait_recv()
        invert_factor(g_own[...] + g_in[it], winv, state)
        for copy in swaps:
            copy.wait_recv()
        if it < ITERS - 1:
            for i in range(tiles):
                both = p_own[tile(i), :] + p_in[it, tile(i), :]
                zt[:, tile(i)] = dot_nt(winv[...], both, precision=HI).astype(B16)
            links.drain()

    half = winv[pl.ds(pl.multiple_of(c * 128, 128), 128), :]
    per_tile = TILE // 64
    for i in range(tiles):
        both = p_own[tile(i), :] + p_in[ITERS - 1, tile(i), :]
        rounded = dot_nt(both, half, precision=HI).astype(B16)
        for b in range(per_tile):
            coef[i * per_tile + b] = rounded[64 * b : 64 * b + 64, :]
    for slot in range(16):
        outbox[slot // 4, 64 * (slot % 4) : 64 * (slot % 4) + 64, :] = coef[order[slot]]
    away = [
        (d, links.start(outbox.at[(x + d) % 4], halves.at[c, x], req=(x + d) % 4))
        for d in (2, 1, 3)
    ]
    halves[c, x] = outbox[x]
    across = [links.start(halves.at[c, x], halves.at[c, x], tp=1 - c)]
    for d, copy in away:
        copy.wait_recv()
        r = (x + 4 - d) % 4
        across.append(links.start(halves.at[c, r], halves.at[c, r], tp=1 - c))
    for copy in across:
        copy.wait_recv()
    for r in range(4):
        out[r, :, :128] = halves[0, r]
        out[r, :, 128:] = halves[1, r]
    links.drain()


def subspace_call(order, keys, basis):
    tokens, width = keys.shape[1], basis.shape[0]
    vm = pltpu.VMEM
    wide = (tokens, 256)
    return pl.pallas_call(
        subspace_kernel,
        out_shape=jax.ShapeDtypeStruct((4, 256, 256), B16),
        in_specs=[
            pl.BlockSpec(memory_space=pltpu.SMEM),
            pl.BlockSpec(memory_space=pl.ANY),
            pl.BlockSpec(memory_space=pl.ANY),
        ],
        out_specs=pl.BlockSpec(memory_space=vm),
        scratch_shapes=[
            vm(keys.shape[1:], B16),
            vm((tokens, width), B16),
            vm((width, 256), B16),
            vm((256, tokens), B16),
            vm(wide, F32),
            vm(wide, F32),
            vm((ITERS,) + wide, F32),
            vm((CHUNKS, 256, FEATS), B16),
            vm((CHUNKS, 128, FEATS), F32),
            vm((CHUNKS, 128, FEATS), F32),
            vm((CHUNKS, 256, FEATS), B16),
            vm((CHUNKS, 256, FEATS), B16),
            vm((CHUNKS, 256, FEATS), F32),
            vm((CHUNKS, 256, FEATS), B16),
            vm((ITERS, CHUNKS, 128, FEATS), B16),
            vm((ITERS, CHUNKS, 128, FEATS), B16),
            vm((ITERS, CHUNKS, 256, FEATS), B16),
            vm((ITERS, CHUNKS, 256, FEATS), B16),
            vm((ITERS, CHUNKS, ZS - 1, PIECE, FEATS), B16),
            vm((ITERS, YS, CHUNKS, 256, FEATS), B16),
            vm((256, 256), F32),
            vm((ITERS, 256, 256), F32),
            vm((256, 256), F32),
            vm((256, 256), F32),
            vm((16, 64, 128), B16),
            vm((4, 256, 128), B16),
            vm((2, 4, 256, 128), B16),
            pltpu.SemaphoreType.DMA((tokens // TILE + 1,)),
            pltpu.SemaphoreType.DMA((COPIES,)),
            pltpu.SemaphoreType.DMA((COPIES,)),
        ],
        compiler_params=pltpu.CompilerParams(
            collective_id=0, has_side_effects=True, vmem_limit_bytes=56 * 2**20
        ),
        name="subspace",
    )(order, keys, basis)


def body(keys, start_basis, owner_map):
    rank = start_basis.shape[-1]
    basis = start_basis.reshape(-1, rank)
    owners = owner_map.reshape(-1)
    slots = jnp.arange(owners.shape[0], dtype=jnp.int32)
    order = jnp.sum(jnp.where(owners[None, :] == slots[:, None], slots[None, :], 0), axis=1)
    handed = subspace_call(order, keys, basis)
    return handed[None, None]


def solution(mesh):
    placed = (
        P("req", "seq", None, "tp", None),
        P("req", None, "tp", None, None),
        P("req", "seq", None),
    )
    return jax.shard_map(
        body,
        mesh=mesh,
        in_specs=placed,
        out_specs=P("req", "seq", None, None, None),
        check_vma=False,
    )
```

```python
import jax
import jax.numpy as jnp
from jax import lax
from jax.experimental import pallas as pl
from jax.experimental.pallas import tpu as pltpu
from jax.sharding import PartitionSpec as P

MESH = pl.DeviceIdType.MESH
HI = lax.Precision.HIGHEST
F32 = jnp.float32
B16 = jnp.bfloat16
YS, ZS = 4, 8
ITERS = 2
TILE = 256
RANK = 256
CHUNKS = 4
B = RANK // CHUNKS
WIDE = 512
EVENTS = 4 + ITERS * (CHUNKS * 8 + 2) + 4
VMEM = 53 * 2**20

PLAN = (
    (0, 0, 0), (0, 0, 1), (0, 1, 0), (0, 0, 2), (0, 1, 1), (0, 0, 3), (0, 2, 0), (0, 1, 2),
    (0, 2, 1), (0, 1, 3), (0, 3, 0), (0, 2, 2), (0, 3, 1), (0, 2, 3), (0, 4, 0), (0, 5, 0),
    (0, 3, 2), (0, 4, 1), (0, 5, 1), (0, 3, 3), (0, 4, 2), (0, 8, 0), (0, 5, 2), (0, 9, 0),
    (0, 6, 0), (0, 7, 0), (1, 0, 0), (0, 4, 3), (0, 5, 3), (0, 6, 1), (0, 7, 1), (1, 0, 1),
    (0, 6, 2), (1, 1, 0), (0, 7, 2), (1, 0, 2), (0, 6, 3), (1, 1, 1), (0, 7, 3), (1, 0, 3),
    (1, 2, 0), (1, 1, 2), (1, 2, 1), (1, 1, 3), (1, 3, 0), (1, 2, 2), (1, 3, 1), (1, 2, 3),
    (1, 4, 0), (1, 5, 0), (1, 3, 2), (1, 4, 1), (1, 5, 1), (1, 3, 3), (1, 4, 2), (1, 5, 2),
    (1, 8, 0), (1, 9, 0), (1, 6, 0), (1, 7, 0), (1, 4, 3), (1, 5, 3), (1, 6, 1), (1, 7, 1),
    (1, 6, 2), (1, 7, 2), (1, 6, 3), (1, 7, 3),
)

def dot_nt(a, b, precision=None):
    return lax.dot_general(
        a, b, (((1,), (1,)), ((), ())), precision=precision, preferred_element_type=F32
    )


def dot_tn(a, b, precision=None):
    return lax.dot_general(
        a, b, (((0,), (0,)), ((), ())), precision=precision, preferred_element_type=F32
    )


def eliminate(block):
    b = block.shape[0]
    low = block
    done = []
    sub = lax.broadcasted_iota(jnp.int32, (8, 128), 0)

    def spread(v, j):
        return jnp.broadcast_to(v[j : j + 1, :], (8, 128))

    def columns(rows, first):
        shape = (rows.shape[0], 128)
        return [jnp.broadcast_to(rows[:, first + j : first + j + 1], shape) for j in range(8)]

    for p in range(b // 8):
        head, low = low[:8], low[8:]
        cols = columns(head, 8 * p)
        below = columns(low, 8 * p) if low.shape[0] else None
        for j in range(0, 8, 2):
            a, edge, d = spread(cols[j], j), spread(cols[j], j + 1), spread(cols[j + 1], j + 1)
            root0 = lax.rsqrt(a)
            inv0 = root0 * root0
            ratio = edge * inv0
            root1 = lax.rsqrt(d - ratio * edge)
            inv1 = root1 * root1
            row0, row1 = spread(head, j), spread(head, j + 1)
            row1 = row1 - ratio * row0
            after = range(j + 2, 8)
            tops0 = {m: spread(cols[m], j) for m in after}
            tops1 = {m: spread(cols[m], j + 1) - ratio * tops0[m] for m in after}
            f0 = jnp.where(sub > j + 1, cols[j] * inv0, 0.0)
            f1 = jnp.where(sub > j + 1, (cols[j + 1] - ratio * cols[j]) * inv1, 0.0)
            head = head - f0 * row0 - f1 * row1
            head = jnp.where(sub == j, row0 * root0, head)
            head = jnp.where(sub == j + 1, row1 * root1, head)
            for m in after:
                cols[m] = cols[m] - f0 * tops0[m] - f1 * tops1[m]
            if below:
                g0 = below[j] * inv0[:1]
                g1 = (below[j + 1] - ratio[:1] * below[j]) * inv1[:1]
                low = low - g0 * row0[:1] - g1 * row1[:1]
                for m in after:
                    below[m] = below[m] - g0 * tops0[m][:1] - g1 * tops1[m][:1]
        done.append(head)
    return jnp.concatenate(done, axis=0)[:, b:]


class Links:
    def __init__(self, send, recv, rows):
        self.send, self.recv, self.rows = send, recv, rows
        self.events, self.bytes, self.sent = {}, [], []

    def start(self, event, src, dst, **device):
        i = self.events.setdefault(event, len(self.events))
        if i == len(self.bytes):
            self.bytes.append(0)
        group = event[0]
        while len(self.sent) <= group:
            self.sent.append(0)
        copy = pltpu.make_async_remote_copy(
            src_ref=src,
            dst_ref=dst,
            send_sem=self.send.at[group],
            recv_sem=self.recv.at[i],
            device_id=device,
            device_id_type=MESH,
        )
        copy.start()
        size = 1
        for extent in src.shape:
            size *= extent
        size *= jnp.dtype(src.dtype).itemsize
        self.bytes[i] += size
        self.sent[group] += size

    def take(self, sem, size):
        height = size // (self.rows.shape[1] * 4)
        part = self.rows.at[pl.ds(0, height)]
        pltpu.make_async_copy(part, part, sem).wait()

    def wait(self, event):
        i = self.events[event]
        self.take(self.recv.at[i], self.bytes[i])

    def drain(self):
        for group, size in enumerate(self.sent):
            self.take(self.send.at[group], size)


def greet(partners):
    barrier = pltpu.get_barrier_semaphore()
    for device in partners:
        pl.semaphore_signal(barrier, inc=1, device_id=device, device_id_type=MESH)


def await_greetings(count):
    pl.semaphore_wait(pltpu.get_barrier_semaphore(), count)


def dot3(a, b):
    ah, bh = a.astype(B16), b.astype(B16)
    al, bl = (a - ah.astype(F32)).astype(B16), (b - bh.astype(F32)).astype(B16)

    def dot(p, q):
        return jnp.dot(p, q, preferred_element_type=F32)

    return dot(ah, bh) + (dot(ah, bl) + dot(al, bh))


def subspace_kernel(
    owners, keys, basis, out,
    raw, k, v0, zt, z_own, z_in, pt, pt_in, opp, right16, left16, own, zsend,
    from_left, from_right, from_far, zin, full, squares, sq_send, sq_yin, sq_tin, trace,
    g_own, g_in, winv, coef, outbox, halves, tally, load, send, recv,
):
    x = lax.axis_index("req")
    s = lax.axis_index("seq")
    c = lax.axis_index("tp")
    y, z = s % YS, s // YS
    links = Links(send, recv, tally)
    tokens = k.shape[0]
    tiles = tokens // TILE

    def at_y(d):
        return z * YS + (y + d) % YS

    def at_z(d):
        return ((z + d) % ZS) * YS + y

    right, left = at_y(1), at_y(3)
    yr, yo, yl = (y + 1) % YS, (y + 2) % YS, (y + 3) % YS
    far_first = (4, 3, 5, 2, 6, 1, 7)

    def tile(i):
        return pl.ds(i * TILE, TILE)

    def piece(d):
        p = (z + d) % ZS
        rows = pl.ds(pl.multiple_of(p // 2 * 16, 16), 16)
        return rows, pl.ds(pl.multiple_of(p % 2 * 256, 256), 256)

    partners = (
        [{"tp": 1 - c}]
        + [{"seq": at_y(d)} for d in range(1, YS)]
        + [{"seq": at_z(d)} for d in range(1, ZS)]
        + [{"req": (x + d) % 4} for d in range(1, 4)]
    )
    loads = [pltpu.make_async_copy(basis, v0, load.at[tiles])]
    for i in range(tiles):
        loads.append(pltpu.make_async_copy(keys.at[0, tile(i)], raw.at[tile(i)], load.at[i]))
    for copy in loads:
        copy.start()
    greet(partners)
    order = {}
    for d in range(4):
        for slot in range(4):
            wanted = (x + d) % 4 * 4 + slot
            block = jnp.int32(0)
            for b in range(16):
                block = jnp.where(owners[b] == wanted, b, block)
            order[d, slot] = block

    loads[0].wait()
    for i in range(tiles):
        loads[1 + i].wait()
        k[tile(i), :] = raw[tile(i)].reshape(TILE, k.shape[1])
        z_own[i] = jnp.dot(k[tile(i), :], v0[...], preferred_element_type=F32)
    await_greetings(len(partners))
    for i in range(tiles):
        links.start((0, "z", i), z_own.at[i], z_in.at[i], tp=1 - c)
    for i in range(tiles):
        links.wait((0, "z", i))
        zt[0, :, tile(i)] = (z_own[i] + z_in[i]).T.astype(B16)

    def iteration(it):
        def cols(q):
            return pl.ds(pl.multiple_of(q * WIDE, WIDE), WIDE)

        def moment(q, j):
            return jnp.dot(
                zt[it, B * j : B * j + B, :], k[:, cols(q)], preferred_element_type=F32
            )

        def start(name, j, src, dst, **device):
            links.start((1 + it, name, j), src, dst, **device)

        def wait(name, j):
            links.wait((1 + it, name, j))

        def reduce0(j):
            opp[it, j] = moment(yo, j).astype(B16)
            start("y", j, opp.at[it, j], from_far.at[it, j], seq=at_y(2))
            right16[it, j] = moment(yr, j).astype(B16)
            start("y", j, right16.at[it, j], from_left.at[it, j], seq=right)
            left16[it, j] = moment(yl, j).astype(B16)
            start("y", j, left16.at[it, j], from_right.at[it, j], seq=left)
            own[j] = moment(y, j)

        def reduce1(j):
            wait("y", j)
            value = own[j] + from_far[it, j].astype(F32)
            value = value + from_left[it, j].astype(F32) + from_right[it, j].astype(F32)
            own[j] = value
            zsend[it, j] = value.astype(B16)
            for d in far_first:
                rows, lanes = piece(d)
                start("z", j, zsend.at[it, j, rows, lanes], zin.at[it, j, d - 1], seq=at_z(d))

        def reduce2(j):
            rows, lanes = piece(0)
            total = own[j, rows, lanes]
            wait("z", j)
            for d in range(1, ZS):
                total = total + zin[it, j, d - 1].astype(F32)
            full[it, j, y, rows, lanes] = total.astype(B16)
            for d in far_first:
                mine = full.at[it, j, y, rows, lanes]
                start("gz", j, mine, mine, seq=at_z(d))

        def absorb(q, j, start=False):
            block = full[it, j, q]
            for i in range(tiles):
                product = dot_nt(block, k[tile(i), cols(q)])
                pt[it, j, :, tile(i)] = product if start else pt[it, j, :, tile(i)] + product
            known = jnp.concatenate([full[it, i, q] for i in range(j + 1)], axis=0)
            product = dot_nt(block, known)
            if j < CHUNKS - 1:
                blank = jnp.zeros((B, RANK - B * (j + 1)), F32)
                product = jnp.concatenate([product, blank], axis=1)
            g_own[it, j] = product if start else g_own[it, j] + product

        def gather0(j):
            wait("gz", j)
            power = jnp.square(full[it, j, y].astype(F32))
            power = jnp.sum(power.reshape(B // 8, 8, WIDE), axis=0)
            power = sum(power[:, 128 * g : 128 * g + 128] for g in range(WIDE // 128))
            squares[it] = power if j == 0 else squares[it] + power
            if j == CHUNKS - 1:
                for d in (2, 1, 3):
                    start("ty", 0, squares.at[it], sq_yin.at[it, d - 1], seq=at_y(d))
            mine = full.at[it, j, y]
            start("go", j, mine, mine, seq=at_y(2))
            start("gr", j, mine, mine, seq=right)
            start("gl", j, mine, mine, seq=left)
            absorb(y, j, start=True)

        def gather1(j):
            wait("gr", j)
            absorb(yl, j)
            wait("gl", j)
            absorb(yr, j)

        def gather2(j):
            wait("go", j)
            absorb(yo, j)
            start("g", j, g_own.at[it, j], g_in.at[it, j], tp=1 - c)
            start("p", j, pt.at[it, j], pt_in.at[it, j], tp=1 - c)

        def trace1(_):
            total = squares[it]
            wait("ty", 0)
            for d in range(1, YS):
                total = total + sq_yin[it, d - 1]
            sq_send[it] = total
            start("tt", 0, sq_send.at[it], sq_tin.at[it], tp=1 - c)

        def trace2(_):
            wait("tt", 0)
            trace[it] = sq_send[it] + sq_tin[it]

        def factor(j):
            lo = B * j
            wait("g", j)
            gram = g_own[it, j] + g_in[it, j]
            shift = 0.0001 * jnp.sum(trace[it]) / RANK
            r = lax.broadcasted_iota(jnp.int32, (B, B), 0)
            l = lax.broadcasted_iota(jnp.int32, (B, B), 1)
            eye = jnp.where(r == l, 1.0, 0.0).astype(F32)
            corner = gram[:, lo : lo + B] + shift * eye
            if j:
                lane = lax.broadcasted_iota(jnp.int32, (B, RANK), 1)
                before = winv[:lo, :]
                row = dot_nt(jnp.where(lane < lo, gram, 0.0), before, precision=HI)
                corner = corner - dot_nt(row, row, precision=HI)
                back = jnp.dot(row, before, precision=HI, preferred_element_type=F32)
            inverse = eliminate(jnp.concatenate([corner, eye], axis=1))
            parts = [jnp.zeros((B, lo), F32)] if lo else []
            parts.append(inverse)
            if lo + B < RANK:
                parts.append(jnp.zeros((B, RANK - lo - B), F32))
            rows = jnp.concatenate(parts, axis=1)
            if j:
                rows = rows - jnp.dot(
                    inverse, back, precision=HI, preferred_element_type=F32
                )
            winv[lo : lo + B, :] = rows

        def project(j):
            wait("p", j)
            pt_in[it, j] = pt[it, j] + pt_in[it, j]
            if it < ITERS - 1:
                known = jnp.concatenate([pt_in[it, i] for i in range(j + 1)], axis=0)
                rows = winv[B * j : B * j + B, : B * (j + 1)]
                zt[it + 1, B * j : B * j + B, :] = dot3(rows, known).astype(B16)

        return (
            reduce0, reduce1, reduce2, gather0, gather1, gather2, factor, project,
            trace1, trace2,
        )

    steps = [iteration(it) for it in range(ITERS)]
    for it, step, j in PLAN:
        steps[it][step](j)

    half = winv[pl.ds(pl.multiple_of(c * 128, 128), 128), :]
    per_tile = TILE // 64
    for i in range(tiles):
        both = jnp.concatenate([pt_in[ITERS - 1, j, :, tile(i)] for j in range(CHUNKS)], axis=0)
        rounded = dot3(half, both).T.astype(B16)
        for b in range(per_tile):
            coef[i * per_tile + b] = rounded[64 * b : 64 * b + 64, :]
    last = 1 + ITERS
    for d in (2, 1, 3, 0):
        rows = jnp.concatenate([coef[order[d, slot]] for slot in range(4)], axis=0)
        if d:
            outbox[d - 1] = rows
            there = halves.at[c, x]
            links.start((last, "x", d), outbox.at[d - 1], there, req=(x + d) % 4)
        else:
            halves[c, x] = rows
    for d in (0, 2, 1, 3):
        r = (x + 4 - d) % 4
        if d:
            links.wait((last, "x", d))
        links.start((last, "c", 0), halves.at[c, r], halves.at[c, r], tp=1 - c)
    links.wait((last, "c", 0))
    for r in range(4):
        out[r, :, :128] = halves[0, r]
        out[r, :, 128:] = halves[1, r]
    links.drain()


def subspace_call(owners, keys, basis):
    tokens, width = keys.shape[1], basis.shape[0]
    vm = pltpu.VMEM
    tiles = tokens // TILE
    every = (ITERS, CHUNKS)
    return pl.pallas_call(
        subspace_kernel,
        out_shape=jax.ShapeDtypeStruct((4, 256, 256), B16),
        in_specs=[
            pl.BlockSpec(memory_space=pltpu.SMEM),
            pl.BlockSpec(memory_space=pl.ANY),
            pl.BlockSpec(memory_space=pl.ANY),
        ],
        out_specs=pl.BlockSpec(memory_space=vm),
        scratch_shapes=[
            vm(keys.shape[1:], B16),
            vm((tokens, width), B16),
            vm((width, RANK), B16),
            vm((ITERS, RANK, tokens), B16),
            vm((tiles, TILE, RANK), F32),
            vm((tiles, TILE, RANK), F32),
            vm(every + (B, tokens), F32),
            vm(every + (B, tokens), F32),
            vm(every + (B, WIDE), B16),
            vm(every + (B, WIDE), B16),
            vm(every + (B, WIDE), B16),
            vm((CHUNKS, B, WIDE), F32),
            vm(every + (B, WIDE), B16),
            vm(every + (B, WIDE), B16),
            vm(every + (B, WIDE), B16),
            vm(every + (B, WIDE), B16),
            vm(every + (ZS - 1, 16, 256), B16),
            vm(every + (YS, B, WIDE), B16),
            vm((ITERS, 8, 128), F32),
            vm((ITERS, 8, 128), F32),
            vm((ITERS, YS - 1, 8, 128), F32),
            vm((ITERS, 8, 128), F32),
            vm((ITERS, 8, 128), F32),
            vm(every + (B, RANK), F32),
            vm(every + (B, RANK), F32),
            vm((RANK, RANK), F32),
            vm((16, 64, 128), B16),
            vm((3, 256, 128), B16),
            vm((2, 4, 256, 128), B16),
            vm((8192, 128), F32),
            pltpu.SemaphoreType.DMA((tiles + 1,)),
            pltpu.SemaphoreType.DMA((2 + ITERS,)),
            pltpu.SemaphoreType.DMA((EVENTS,)),
        ],
        compiler_params=pltpu.CompilerParams(
            collective_id=0, has_side_effects=True, vmem_limit_bytes=VMEM
        ),
        name="subspace",
    )(owners, keys, basis)


def body(keys, start_basis, owner_map):
    basis = start_basis.reshape(-1, start_basis.shape[-1])
    handed = subspace_call(owner_map.reshape(-1), keys, basis)
    return handed[None, None]


def solution(mesh):
    placed = (
        P("req", "seq", None, "tp", None),
        P("req", None, "tp", None, None),
        P("req", "seq", None),
    )
    return jax.shard_map(
        body,
        mesh=mesh,
        in_specs=placed,
        out_specs=P("req", "seq", None, None, None),
        check_vma=False,
    )
```

```python
import jax
import jax.numpy as jnp
from jax import lax
from jax.experimental import pallas as pl
from jax.experimental.pallas import tpu as pltpu
from jax.sharding import PartitionSpec as P

MESH = pl.DeviceIdType.MESH
HI = lax.Precision.HIGHEST
F32 = jnp.float32
B16 = jnp.bfloat16
YS, ZS = 4, 8
ITERS = 2
TILE = 256
RANK = 256
CHUNKS = 4
B = RANK // CHUNKS
WIDE = 512
EVENTS = 4 + ITERS * (CHUNKS * 8 + 2) + 8
VMEM = 53 * 2**20

PLAN = (
    (0, 0, 0), (0, 0, 1), (0, 0, 2), (0, 1, 0), (0, 0, 3), (0, 1, 1), (0, 2, 0), (0, 1, 2),
    (0, 2, 1), (0, 1, 3), (0, 3, 0), (0, 2, 2), (0, 3, 1), (0, 2, 3), (0, 3, 2), (0, 4, 0),
    (0, 5, 0), (0, 3, 3), (0, 4, 1), (0, 5, 1), (0, 8, 0), (0, 9, 0), (0, 6, 0), (0, 7, 0),
    (1, 0, 0), (0, 4, 2), (0, 5, 2), (0, 4, 3), (0, 5, 3), (0, 6, 1), (1, 1, 0), (0, 7, 1),
    (1, 0, 1), (0, 6, 2), (0, 7, 2), (1, 0, 2), (0, 6, 3), (1, 1, 1), (1, 2, 0), (0, 7, 3),
    (1, 0, 3), (1, 1, 2), (1, 2, 1), (1, 1, 3), (1, 3, 0), (1, 2, 2), (1, 3, 1), (1, 2, 3),
    (1, 3, 2), (1, 4, 0), (1, 5, 0), (1, 3, 3), (1, 4, 1), (1, 5, 1), (1, 8, 0), (1, 9, 0),
    (1, 4, 2), (1, 5, 2), (1, 6, 0), (1, 7, 0), (1, 6, 1), (1, 7, 1), (1, 10, 0), (1, 4, 3),
    (1, 5, 3), (1, 6, 2), (1, 11, 0), (1, 7, 2), (1, 6, 3), (1, 7, 3), (1, 10, 1), (1, 12, 0),
    (1, 11, 1), (1, 12, 1),
)

def dot_nt(a, b, precision=None):
    return lax.dot_general(
        a, b, (((1,), (1,)), ((), ())), precision=precision, preferred_element_type=F32
    )


def dot_tn(a, b, precision=None):
    return lax.dot_general(
        a, b, (((0,), (0,)), ((), ())), precision=precision, preferred_element_type=F32
    )


def eliminate(block):
    b = block.shape[0]
    low = block
    done = []
    sub = lax.broadcasted_iota(jnp.int32, (8, 128), 0)

    def spread(v, j):
        return jnp.broadcast_to(v[j : j + 1, :], (8, 128))

    def columns(rows, first):
        shape = (rows.shape[0], 128)
        return [jnp.broadcast_to(rows[:, first + j : first + j + 1], shape) for j in range(8)]

    for p in range(b // 8):
        head, low = low[:8], low[8:]
        cols = columns(head, 8 * p)
        below = columns(low, 8 * p) if low.shape[0] else None
        for j in range(0, 8, 2):
            a, edge, d = spread(cols[j], j), spread(cols[j], j + 1), spread(cols[j + 1], j + 1)
            root0 = lax.rsqrt(a)
            inv0 = root0 * root0
            ratio = edge * inv0
            root1 = lax.rsqrt(d - ratio * edge)
            inv1 = root1 * root1
            row0, row1 = spread(head, j), spread(head, j + 1)
            row1 = row1 - ratio * row0
            after = range(j + 2, 8)
            tops0 = {m: spread(cols[m], j) for m in after}
            tops1 = {m: spread(cols[m], j + 1) - ratio * tops0[m] for m in after}
            f0 = jnp.where(sub > j + 1, cols[j] * inv0, 0.0)
            f1 = jnp.where(sub > j + 1, (cols[j + 1] - ratio * cols[j]) * inv1, 0.0)
            head = head - f0 * row0 - f1 * row1
            head = jnp.where(sub == j, row0 * root0, head)
            head = jnp.where(sub == j + 1, row1 * root1, head)
            for m in after:
                cols[m] = cols[m] - f0 * tops0[m] - f1 * tops1[m]
            if below:
                g0 = below[j] * inv0[:1]
                g1 = (below[j + 1] - ratio[:1] * below[j]) * inv1[:1]
                low = low - g0 * row0[:1] - g1 * row1[:1]
                for m in after:
                    below[m] = below[m] - g0 * tops0[m][:1] - g1 * tops1[m][:1]
        done.append(head)
    return jnp.concatenate(done, axis=0)[:, b:]


class Links:
    def __init__(self, send, recv, rows):
        self.send, self.recv, self.rows = send, recv, rows
        self.events, self.bytes, self.sent = {}, [], []

    def start(self, event, src, dst, **device):
        i = self.events.setdefault(event, len(self.events))
        if i == len(self.bytes):
            self.bytes.append(0)
        group = event[0]
        while len(self.sent) <= group:
            self.sent.append(0)
        copy = pltpu.make_async_remote_copy(
            src_ref=src,
            dst_ref=dst,
            send_sem=self.send.at[group],
            recv_sem=self.recv.at[i],
            device_id=device,
            device_id_type=MESH,
        )
        copy.start()
        size = 1
        for extent in src.shape:
            size *= extent
        size *= jnp.dtype(src.dtype).itemsize
        self.bytes[i] += size
        self.sent[group] += size

    def take(self, sem, size):
        height = size // (self.rows.shape[1] * 4)
        part = self.rows.at[pl.ds(0, height)]
        pltpu.make_async_copy(part, part, sem).wait()

    def wait(self, event):
        i = self.events[event]
        self.take(self.recv.at[i], self.bytes[i])

    def drain(self):
        for group, size in enumerate(self.sent):
            self.take(self.send.at[group], size)


def greet(partners):
    barrier = pltpu.get_barrier_semaphore()
    for device in partners:
        pl.semaphore_signal(barrier, inc=1, device_id=device, device_id_type=MESH)


def await_greetings(count):
    pl.semaphore_wait(pltpu.get_barrier_semaphore(), count)


def dot3(a, b):
    ah, bh = a.astype(B16), b.astype(B16)
    al, bl = (a - ah.astype(F32)).astype(B16), (b - bh.astype(F32)).astype(B16)

    def dot(p, q):
        return jnp.dot(p, q, preferred_element_type=F32)

    return dot(ah, bh) + (dot(ah, bl) + dot(al, bh))


def subspace_kernel(
    owners, keys, basis, out,
    raw, k, v0, zt, z_own, z_in, pt, pt_in, opp, right16, left16, own, zsend,
    from_left, from_right, from_far, zin, full, squares, sq_send, sq_yin, sq_tin, trace,
    g_own, g_in, winv, coef, outbox, halves, tally, load, send, recv,
):
    x = lax.axis_index("req")
    s = lax.axis_index("seq")
    c = lax.axis_index("tp")
    y, z = s % YS, s // YS
    links = Links(send, recv, tally)
    tokens = k.shape[0]
    tiles = tokens // TILE

    def at_y(d):
        return z * YS + (y + d) % YS

    def at_z(d):
        return ((z + d) % ZS) * YS + y

    right, left = at_y(1), at_y(3)
    yr, yo, yl = (y + 1) % YS, (y + 2) % YS, (y + 3) % YS
    far_first = (4, 3, 5, 2, 6, 1, 7)

    def tile(i):
        return pl.ds(i * TILE, TILE)

    def piece(d):
        p = (z + d) % ZS
        rows = pl.ds(pl.multiple_of(p // 2 * 16, 16), 16)
        return rows, pl.ds(pl.multiple_of(p % 2 * 256, 256), 256)

    partners = (
        [{"tp": 1 - c}]
        + [{"seq": at_y(d)} for d in range(1, YS)]
        + [{"seq": at_z(d)} for d in range(1, ZS)]
        + [{"req": (x + d) % 4} for d in range(1, 4)]
    )
    loads = [pltpu.make_async_copy(basis, v0, load.at[tiles])]
    for i in range(tiles):
        loads.append(pltpu.make_async_copy(keys.at[0, tile(i)], raw.at[tile(i)], load.at[i]))
    for copy in loads:
        copy.start()
    greet(partners)
    order = {}
    for d in range(4):
        for t in range(2):
            wanted = (x + d) % 4 * 4 + 2 * c + t
            block = jnp.int32(0)
            for b in range(16):
                block = jnp.where(owners[b] == wanted, b, block)
            order[d, t] = block

    loads[0].wait()
    for i in range(tiles):
        loads[1 + i].wait()
        k[tile(i), :] = raw[tile(i)].reshape(TILE, k.shape[1])
        value = jnp.dot(k[tile(i), :], v0[...], preferred_element_type=F32).T
        for j in range(CHUNKS):
            z_own[j, :, tile(i)] = value[B * j : B * j + B]
    await_greetings(len(partners))
    for j in range(CHUNKS):
        links.start((0, "z", j), z_own.at[j], z_in.at[j], tp=1 - c)

    def iteration(it):
        def cols(q):
            return pl.ds(pl.multiple_of(q * WIDE, WIDE), WIDE)

        def moment(q, j):
            return jnp.dot(
                zt[it, B * j : B * j + B, :], k[:, cols(q)], preferred_element_type=F32
            )

        def start(name, j, src, dst, **device):
            links.start((1 + it, name, j), src, dst, **device)

        def wait(name, j):
            links.wait((1 + it, name, j))

        def reduce0(j):
            if it == 0:
                links.wait((0, "z", j))
                zt[0, B * j : B * j + B, :] = (z_own[j] + z_in[j]).astype(B16)
            opp[it, j] = moment(yo, j).astype(B16)
            start("y", j, opp.at[it, j], from_far.at[it, j], seq=at_y(2))
            right16[it, j] = moment(yr, j).astype(B16)
            start("y", j, right16.at[it, j], from_left.at[it, j], seq=right)
            left16[it, j] = moment(yl, j).astype(B16)
            start("y", j, left16.at[it, j], from_right.at[it, j], seq=left)
            own[j] = moment(y, j)

        def reduce1(j):
            wait("y", j)
            value = own[j] + from_far[it, j].astype(F32)
            value = value + from_left[it, j].astype(F32) + from_right[it, j].astype(F32)
            own[j] = value
            zsend[it, j] = value.astype(B16)
            for d in far_first:
                rows, lanes = piece(d)
                start("z", j, zsend.at[it, j, rows, lanes], zin.at[it, j, d - 1], seq=at_z(d))

        def reduce2(j):
            rows, lanes = piece(0)
            total = own[j, rows, lanes]
            wait("z", j)
            for d in range(1, ZS):
                total = total + zin[it, j, d - 1].astype(F32)
            full[it, j, y, rows, lanes] = total.astype(B16)
            for d in far_first:
                mine = full.at[it, j, y, rows, lanes]
                start("gz", j, mine, mine, seq=at_z(d))

        def absorb(q, j, start=False):
            block = full[it, j, q]
            for i in range(tiles):
                product = dot_nt(block, k[tile(i), cols(q)])
                pt[it, j, :, tile(i)] = product if start else pt[it, j, :, tile(i)] + product
            known = jnp.concatenate([full[it, i, q] for i in range(j + 1)], axis=0)
            product = dot_nt(block, known)
            if j < CHUNKS - 1:
                blank = jnp.zeros((B, RANK - B * (j + 1)), F32)
                product = jnp.concatenate([product, blank], axis=1)
            g_own[it, j] = product if start else g_own[it, j] + product

        def gather0(j):
            wait("gz", j)
            power = jnp.square(full[it, j, y].astype(F32))
            power = jnp.sum(power.reshape(B // 8, 8, WIDE), axis=0)
            power = sum(power[:, 128 * g : 128 * g + 128] for g in range(WIDE // 128))
            squares[it] = power if j == 0 else squares[it] + power
            if j == CHUNKS - 1:
                for d in (2, 1, 3):
                    start("ty", 0, squares.at[it], sq_yin.at[it, d - 1], seq=at_y(d))
            mine = full.at[it, j, y]
            start("go", j, mine, mine, seq=at_y(2))
            start("gr", j, mine, mine, seq=right)
            start("gl", j, mine, mine, seq=left)
            absorb(y, j, start=True)

        def gather1(j):
            wait("gr", j)
            absorb(yl, j)
            wait("gl", j)
            absorb(yr, j)

        def gather2(j):
            wait("go", j)
            absorb(yo, j)
            start("g", j, g_own.at[it, j], g_in.at[it, j], tp=1 - c)
            start("p", j, pt.at[it, j], pt_in.at[it, j], tp=1 - c)

        def trace1(_):
            total = squares[it]
            wait("ty", 0)
            for d in range(1, YS):
                total = total + sq_yin[it, d - 1]
            sq_send[it] = total
            start("tt", 0, sq_send.at[it], sq_tin.at[it], tp=1 - c)

        def trace2(_):
            wait("tt", 0)
            trace[it] = sq_send[it] + sq_tin[it]

        def factor(j):
            lo = B * j
            wait("g", j)
            gram = g_own[it, j] + g_in[it, j]
            shift = 0.0001 * jnp.sum(trace[it]) / RANK
            r = lax.broadcasted_iota(jnp.int32, (B, B), 0)
            l = lax.broadcasted_iota(jnp.int32, (B, B), 1)
            eye = jnp.where(r == l, 1.0, 0.0).astype(F32)
            corner = gram[:, lo : lo + B] + shift * eye
            if j:
                lane = lax.broadcasted_iota(jnp.int32, (B, RANK), 1)
                before = winv[:lo, :]
                row = dot_nt(jnp.where(lane < lo, gram, 0.0), before, precision=HI)
                corner = corner - dot_nt(row, row, precision=HI)
                back = jnp.dot(row, before, precision=HI, preferred_element_type=F32)
            inverse = eliminate(jnp.concatenate([corner, eye], axis=1))
            parts = [jnp.zeros((B, lo), F32)] if lo else []
            parts.append(inverse)
            if lo + B < RANK:
                parts.append(jnp.zeros((B, RANK - lo - B), F32))
            rows = jnp.concatenate(parts, axis=1)
            if j:
                rows = rows - jnp.dot(
                    inverse, back, precision=HI, preferred_element_type=F32
                )
            winv[lo : lo + B, :] = rows

        def project(j):
            wait("p", j)
            pt_in[it, j] = pt[it, j] + pt_in[it, j]
            if it < ITERS - 1:
                known = jnp.concatenate([pt_in[it, i] for i in range(j + 1)], axis=0)
                rows = winv[B * j : B * j + B, : B * (j + 1)]
                zt[it + 1, B * j : B * j + B, :] = dot3(rows, known).astype(B16)

        last = 1 + ITERS
        slots = pl.ds(2 * c, 2)

        def hand0(h):
            lo, hi = 128 * h, 128 * h + 128
            rows = winv[lo:hi, :hi]
            for i in range(tiles):
                known = [pt_in[it, j, :, tile(i)] for j in range(hi // B)]
                rounded = dot3(rows, jnp.concatenate(known, axis=0)).T.astype(B16)
                for b in range(TILE // 64):
                    coef[h, i * (TILE // 64) + b] = rounded[64 * b : 64 * b + 64, :]
            for d in (2, 1, 3, 0):
                for t in range(2):
                    if d:
                        outbox[h, d - 1, t] = coef[h, order[d, t]]
                    else:
                        halves[h, x, 2 * c + t] = coef[h, order[d, t]]
                if d:
                    there = halves.at[h, x, slots]
                    links.start((last, h, d), outbox.at[h, d - 1], there, req=(x + d) % 4)

        def hand1(h):
            for d in (0, 2, 1, 3):
                r = (x + 4 - d) % 4
                if d:
                    links.wait((last, h, d))
                mine = halves.at[h, r, slots]
                links.start((last, h, 0), mine, mine, tp=1 - c)

        def hand2(h):
            links.wait((last, h, 0))
            for r in range(4):
                for slot in range(4):
                    out[r, 64 * slot : 64 * slot + 64, 128 * h : 128 * h + 128] = halves[h, r, slot]

        return (
            reduce0, reduce1, reduce2, gather0, gather1, gather2, factor, project,
            trace1, trace2, hand0, hand1, hand2,
        )

    steps = [iteration(it) for it in range(ITERS)]
    for it, step, j in PLAN:
        steps[it][step](j)

    links.drain()


def subspace_call(owners, keys, basis):
    tokens, width = keys.shape[1], basis.shape[0]
    vm = pltpu.VMEM
    tiles = tokens // TILE
    every = (ITERS, CHUNKS)
    return pl.pallas_call(
        subspace_kernel,
        out_shape=jax.ShapeDtypeStruct((4, 256, 256), B16),
        in_specs=[
            pl.BlockSpec(memory_space=pltpu.SMEM),
            pl.BlockSpec(memory_space=pl.ANY),
            pl.BlockSpec(memory_space=pl.ANY),
        ],
        out_specs=pl.BlockSpec(memory_space=vm),
        scratch_shapes=[
            vm(keys.shape[1:], B16),
            vm((tokens, width), B16),
            vm((width, RANK), B16),
            vm((ITERS, RANK, tokens), B16),
            vm((CHUNKS, B, tokens), F32),
            vm((CHUNKS, B, tokens), F32),
            vm(every + (B, tokens), F32),
            vm(every + (B, tokens), F32),
            vm(every + (B, WIDE), B16),
            vm(every + (B, WIDE), B16),
            vm(every + (B, WIDE), B16),
            vm((CHUNKS, B, WIDE), F32),
            vm(every + (B, WIDE), B16),
            vm(every + (B, WIDE), B16),
            vm(every + (B, WIDE), B16),
            vm(every + (B, WIDE), B16),
            vm(every + (ZS - 1, 16, 256), B16),
            vm(every + (YS, B, WIDE), B16),
            vm((ITERS, 8, 128), F32),
            vm((ITERS, 8, 128), F32),
            vm((ITERS, YS - 1, 8, 128), F32),
            vm((ITERS, 8, 128), F32),
            vm((ITERS, 8, 128), F32),
            vm(every + (B, RANK), F32),
            vm(every + (B, RANK), F32),
            vm((RANK, RANK), F32),
            vm((2, 16, 64, 128), B16),
            vm((2, 3, 2, 64, 128), B16),
            vm((2, 4, 4, 64, 128), B16),
            vm((8192, 128), F32),
            pltpu.SemaphoreType.DMA((tiles + 1,)),
            pltpu.SemaphoreType.DMA((2 + ITERS,)),
            pltpu.SemaphoreType.DMA((EVENTS,)),
        ],
        compiler_params=pltpu.CompilerParams(
            collective_id=0, has_side_effects=True, vmem_limit_bytes=VMEM
        ),
        name="subspace",
    )(owners, keys, basis)


def body(keys, start_basis, owner_map):
    basis = start_basis.reshape(-1, start_basis.shape[-1])
    handed = subspace_call(owner_map.reshape(-1), keys, basis)
    return handed[None, None]


def solution(mesh):
    placed = (
        P("req", "seq", None, "tp", None),
        P("req", None, "tp", None, None),
        P("req", "seq", None),
    )
    return jax.shard_map(
        body,
        mesh=mesh,
        in_specs=placed,
        out_specs=P("req", "seq", None, None, None),
        check_vma=False,
    )
```

```python
import jax
import jax.numpy as jnp
from jax import lax
from jax.experimental import pallas as pl
from jax.experimental.pallas import tpu as pltpu
from jax.sharding import PartitionSpec as P

MESH = pl.DeviceIdType.MESH
HI = lax.Precision.HIGHEST
F32 = jnp.float32
B16 = jnp.bfloat16
YS, ZS = 4, 8
ITERS = 2
TILE = 256
RANK = 256
CHUNKS = 4
B = RANK // CHUNKS
WIDE = 512
EVENTS = 4 + ITERS * (CHUNKS * 8 + 1) + 8
VMEM = 53 * 2**20

PLAN = (
    (0, 0, 0), (0, 0, 1), (0, 0, 2), (0, 1, 0), (0, 0, 3), (0, 1, 1), (0, 2, 0), (0, 1, 2),
    (0, 2, 1), (0, 1, 3), (0, 3, 0), (0, 2, 2), (0, 3, 1), (0, 2, 3), (0, 3, 2), (0, 4, 0),
    (0, 5, 0), (0, 3, 3), (0, 4, 1), (0, 5, 1), (0, 8, 0), (0, 6, 0), (0, 7, 0), (1, 0, 0),
    (0, 4, 2), (0, 5, 2), (0, 4, 3), (0, 5, 3), (0, 6, 1), (1, 1, 0), (0, 7, 1), (1, 0, 1),
    (0, 6, 2), (0, 7, 2), (1, 0, 2), (0, 6, 3), (1, 1, 1), (1, 2, 0), (0, 7, 3), (1, 0, 3),
    (1, 1, 2), (1, 2, 1), (1, 1, 3), (1, 3, 0), (1, 2, 2), (1, 3, 1), (1, 2, 3), (1, 3, 2),
    (1, 4, 0), (1, 5, 0), (1, 3, 3), (1, 4, 1), (1, 5, 1), (1, 8, 0), (1, 4, 2), (1, 5, 2),
    (1, 6, 0), (1, 7, 0), (1, 6, 1), (1, 7, 1), (1, 9, 0), (1, 4, 3), (1, 5, 3), (1, 6, 2),
    (1, 10, 0), (1, 7, 2), (1, 6, 3), (1, 7, 3), (1, 9, 1), (1, 11, 0), (1, 10, 1), (1, 11, 1),
)

def dot_nt(a, b, precision=None):
    return lax.dot_general(
        a, b, (((1,), (1,)), ((), ())), precision=precision, preferred_element_type=F32
    )


def dot_tn(a, b, precision=None):
    return lax.dot_general(
        a, b, (((0,), (0,)), ((), ())), precision=precision, preferred_element_type=F32
    )


def eliminate(block):
    b = block.shape[0]
    low = block
    done = []
    sub = lax.broadcasted_iota(jnp.int32, (8, 128), 0)

    def spread(v, j):
        return jnp.broadcast_to(v[j : j + 1, :], (8, 128))

    def columns(rows, first):
        shape = (rows.shape[0], 128)
        return [jnp.broadcast_to(rows[:, first + j : first + j + 1], shape) for j in range(8)]

    for p in range(b // 8):
        head, low = low[:8], low[8:]
        cols = columns(head, 8 * p)
        below = columns(low, 8 * p) if low.shape[0] else None
        for j in range(0, 8, 2):
            a, edge, d = spread(cols[j], j), spread(cols[j], j + 1), spread(cols[j + 1], j + 1)
            root0 = lax.rsqrt(a)
            inv0 = root0 * root0
            ratio = edge * inv0
            root1 = lax.rsqrt(d - ratio * edge)
            inv1 = root1 * root1
            row0, row1 = spread(head, j), spread(head, j + 1)
            row1 = row1 - ratio * row0
            after = range(j + 2, 8)
            tops0 = {m: spread(cols[m], j) for m in after}
            tops1 = {m: spread(cols[m], j + 1) - ratio * tops0[m] for m in after}
            f0 = jnp.where(sub > j + 1, cols[j] * inv0, 0.0)
            f1 = jnp.where(sub > j + 1, (cols[j + 1] - ratio * cols[j]) * inv1, 0.0)
            head = head - f0 * row0 - f1 * row1
            head = jnp.where(sub == j, row0 * root0, head)
            head = jnp.where(sub == j + 1, row1 * root1, head)
            for m in after:
                cols[m] = cols[m] - f0 * tops0[m] - f1 * tops1[m]
            if below:
                g0 = below[j] * inv0[:1]
                g1 = (below[j + 1] - ratio[:1] * below[j]) * inv1[:1]
                low = low - g0 * row0[:1] - g1 * row1[:1]
                for m in after:
                    below[m] = below[m] - g0 * tops0[m][:1] - g1 * tops1[m][:1]
        done.append(head)
    return jnp.concatenate(done, axis=0)[:, b:]


class Links:
    def __init__(self, send, recv, rows):
        self.send, self.recv, self.rows = send, recv, rows
        self.events, self.bytes, self.sent = {}, [], []

    def start(self, event, src, dst, **device):
        i = self.events.setdefault(event, len(self.events))
        if i == len(self.bytes):
            self.bytes.append(0)
        group = event[0]
        while len(self.sent) <= group:
            self.sent.append(0)
        copy = pltpu.make_async_remote_copy(
            src_ref=src,
            dst_ref=dst,
            send_sem=self.send.at[group],
            recv_sem=self.recv.at[i],
            device_id=device,
            device_id_type=MESH,
        )
        copy.start()
        size = 1
        for extent in src.shape:
            size *= extent
        size *= jnp.dtype(src.dtype).itemsize
        self.bytes[i] += size
        self.sent[group] += size

    def take(self, sem, size):
        height = size // (self.rows.shape[1] * 4)
        part = self.rows.at[pl.ds(0, height)]
        pltpu.make_async_copy(part, part, sem).wait()

    def wait(self, event):
        i = self.events[event]
        self.take(self.recv.at[i], self.bytes[i])

    def drain(self):
        for group, size in enumerate(self.sent):
            self.take(self.send.at[group], size)


def greet(partners):
    barrier = pltpu.get_barrier_semaphore()
    for device in partners:
        pl.semaphore_signal(barrier, inc=1, device_id=device, device_id_type=MESH)


def await_greetings(count):
    pl.semaphore_wait(pltpu.get_barrier_semaphore(), count)


def dot3(a, b):
    ah, bh = a.astype(B16), b.astype(B16)
    al, bl = (a - ah.astype(F32)).astype(B16), (b - bh.astype(F32)).astype(B16)

    def dot(p, q):
        return jnp.dot(p, q, preferred_element_type=F32)

    return dot(ah, bh) + (dot(ah, bl) + dot(al, bh))


def subspace_kernel(
    owners, keys, basis, out,
    raw, k, v0, zt, z_own, z_in, pt, pt_in, opp, right16, left16, own, zsend,
    from_left, from_right, from_far, zin, full, squares, sq_in, trace,
    g_own, g_in, winv, coef, outbox, halves, tally, load, send, recv,
):
    x = lax.axis_index("req")
    s = lax.axis_index("seq")
    c = lax.axis_index("tp")
    y, z = s % YS, s // YS
    links = Links(send, recv, tally)
    tokens = k.shape[0]
    tiles = tokens // TILE

    def at_y(d):
        return z * YS + (y + d) % YS

    def at_z(d):
        return ((z + d) % ZS) * YS + y

    right, left = at_y(1), at_y(3)
    yr, yo, yl = (y + 1) % YS, (y + 2) % YS, (y + 3) % YS
    far_first = (4, 3, 5, 2, 6, 1, 7)

    def tile(i):
        return pl.ds(i * TILE, TILE)

    def piece(d):
        p = (z + d) % ZS
        rows = pl.ds(pl.multiple_of(p // 2 * 16, 16), 16)
        return rows, pl.ds(pl.multiple_of(p % 2 * 256, 256), 256)

    partners = (
        [{"tp": 1 - c}]
        + [{"seq": at_y(d)} for d in range(1, YS)]
        + [{"seq": at_y(d), "tp": 1 - c} for d in range(1, YS)]
        + [{"seq": at_z(d)} for d in range(1, ZS)]
        + [{"req": (x + d) % 4} for d in range(1, 4)]
    )
    loads = [pltpu.make_async_copy(basis, v0, load.at[tiles])]
    for i in range(tiles):
        loads.append(pltpu.make_async_copy(keys.at[0, tile(i)], raw.at[tile(i)], load.at[i]))
    for copy in loads:
        copy.start()
    greet(partners)
    order = {}
    for d in range(4):
        for t in range(2):
            wanted = (x + d) % 4 * 4 + 2 * c + t
            block = jnp.int32(0)
            for b in range(16):
                block = jnp.where(owners[b] == wanted, b, block)
            order[d, t] = block

    loads[0].wait()
    for i in range(tiles):
        loads[1 + i].wait()
        k[tile(i), :] = raw[tile(i)].reshape(TILE, k.shape[1])
        value = jnp.dot(k[tile(i), :], v0[...], preferred_element_type=F32).T
        for j in range(CHUNKS):
            z_own[j, :, tile(i)] = value[B * j : B * j + B]
    await_greetings(len(partners))
    for j in range(CHUNKS):
        links.start((0, "z", j), z_own.at[j], z_in.at[j], tp=1 - c)

    def iteration(it):
        def cols(q):
            return pl.ds(pl.multiple_of(q * WIDE, WIDE), WIDE)

        def moment(q, j):
            return jnp.dot(
                zt[it, B * j : B * j + B, :], k[:, cols(q)], preferred_element_type=F32
            )

        def start(name, j, src, dst, **device):
            links.start((1 + it, name, j), src, dst, **device)

        def wait(name, j):
            links.wait((1 + it, name, j))

        def reduce0(j):
            if it == 0:
                links.wait((0, "z", j))
                zt[0, B * j : B * j + B, :] = (z_own[j] + z_in[j]).astype(B16)
            opp[it, j] = moment(yo, j).astype(B16)
            start("y", j, opp.at[it, j], from_far.at[it, j], seq=at_y(2))
            right16[it, j] = moment(yr, j).astype(B16)
            start("y", j, right16.at[it, j], from_left.at[it, j], seq=right)
            left16[it, j] = moment(yl, j).astype(B16)
            start("y", j, left16.at[it, j], from_right.at[it, j], seq=left)
            own[j] = moment(y, j)

        def reduce1(j):
            wait("y", j)
            value = own[j] + from_far[it, j].astype(F32)
            value = value + from_left[it, j].astype(F32) + from_right[it, j].astype(F32)
            own[j] = value
            zsend[it, j] = value.astype(B16)
            for d in far_first:
                rows, lanes = piece(d)
                start("z", j, zsend.at[it, j, rows, lanes], zin.at[it, j, d - 1], seq=at_z(d))

        def reduce2(j):
            rows, lanes = piece(0)
            total = own[j, rows, lanes]
            wait("z", j)
            for d in range(1, ZS):
                total = total + zin[it, j, d - 1].astype(F32)
            full[it, j, y, rows, lanes] = total.astype(B16)
            for d in far_first:
                mine = full.at[it, j, y, rows, lanes]
                start("gz", j, mine, mine, seq=at_z(d))

        def absorb(q, j, start=False):
            block = full[it, j, q]
            for i in range(tiles):
                product = dot_nt(block, k[tile(i), cols(q)])
                pt[it, j, :, tile(i)] = product if start else pt[it, j, :, tile(i)] + product
            known = jnp.concatenate([full[it, i, q] for i in range(j + 1)], axis=0)
            product = dot_nt(block, known)
            if j < CHUNKS - 1:
                blank = jnp.zeros((B, RANK - B * (j + 1)), F32)
                product = jnp.concatenate([product, blank], axis=1)
            g_own[it, j] = product if start else g_own[it, j] + product

        def gather0(j):
            wait("gz", j)
            power = jnp.square(full[it, j, y].astype(F32))
            power = jnp.sum(power.reshape(B // 8, 8, WIDE), axis=0)
            power = sum(power[:, 128 * g : 128 * g + 128] for g in range(WIDE // 128))
            squares[it] = power if j == 0 else squares[it] + power
            if j == CHUNKS - 1:
                sq_in[it, YS * c + y] = squares[it]
                there = sq_in.at[it, YS * c + y]
                for d in (2, 1, 3):
                    start("t", 0, squares.at[it], there, seq=at_y(d))
                    start("t", 0, squares.at[it], there, seq=at_y(d), tp=1 - c)
                start("t", 0, squares.at[it], there, tp=1 - c)
            mine = full.at[it, j, y]
            start("go", j, mine, mine, seq=at_y(2))
            start("gr", j, mine, mine, seq=right)
            start("gl", j, mine, mine, seq=left)
            absorb(y, j, start=True)

        def gather1(j):
            wait("gr", j)
            absorb(yl, j)
            wait("gl", j)
            absorb(yr, j)

        def gather2(j):
            wait("go", j)
            absorb(yo, j)
            start("g", j, g_own.at[it, j], g_in.at[it, j], tp=1 - c)
            start("p", j, pt.at[it, j], pt_in.at[it, j], tp=1 - c)

        def trace1(_):
            wait("t", 0)
            total = sq_in[it, 0]
            for i in range(1, 2 * YS):
                total = total + sq_in[it, i]
            trace[it] = total

        def factor(j):
            lo = B * j
            wait("g", j)
            gram = g_own[it, j] + g_in[it, j]
            shift = 0.0001 * jnp.sum(trace[it]) / RANK
            r = lax.broadcasted_iota(jnp.int32, (B, B), 0)
            l = lax.broadcasted_iota(jnp.int32, (B, B), 1)
            eye = jnp.where(r == l, 1.0, 0.0).astype(F32)
            corner = gram[:, lo : lo + B] + shift * eye
            if j:
                lane = lax.broadcasted_iota(jnp.int32, (B, RANK), 1)
                before = winv[:lo, :]
                row = dot_nt(jnp.where(lane < lo, gram, 0.0), before, precision=HI)
                corner = corner - dot_nt(row, row, precision=HI)
                back = jnp.dot(row, before, precision=HI, preferred_element_type=F32)
            inverse = eliminate(jnp.concatenate([corner, eye], axis=1))
            parts = [jnp.zeros((B, lo), F32)] if lo else []
            parts.append(inverse)
            if lo + B < RANK:
                parts.append(jnp.zeros((B, RANK - lo - B), F32))
            rows = jnp.concatenate(parts, axis=1)
            if j:
                rows = rows - jnp.dot(
                    inverse, back, precision=HI, preferred_element_type=F32
                )
            winv[lo : lo + B, :] = rows

        def project(j):
            wait("p", j)
            pt_in[it, j] = pt[it, j] + pt_in[it, j]
            if it < ITERS - 1:
                known = jnp.concatenate([pt_in[it, i] for i in range(j + 1)], axis=0)
                rows = winv[B * j : B * j + B, : B * (j + 1)]
                zt[it + 1, B * j : B * j + B, :] = dot3(rows, known).astype(B16)

        last = 1 + ITERS
        slots = pl.ds(2 * c, 2)

        def hand0(h):
            lo, hi = 128 * h, 128 * h + 128
            rows = winv[lo:hi, :hi]
            for i in range(tiles):
                known = [pt_in[it, j, :, tile(i)] for j in range(hi // B)]
                rounded = dot3(rows, jnp.concatenate(known, axis=0)).T.astype(B16)
                for b in range(TILE // 64):
                    coef[h, i * (TILE // 64) + b] = rounded[64 * b : 64 * b + 64, :]
            for d in (2, 1, 3, 0):
                for t in range(2):
                    if d:
                        outbox[h, d - 1, t] = coef[h, order[d, t]]
                    else:
                        halves[h, x, 2 * c + t] = coef[h, order[d, t]]
                if d:
                    there = halves.at[h, x, slots]
                    links.start((last, h, d), outbox.at[h, d - 1], there, req=(x + d) % 4)

        def hand1(h):
            for d in (0, 2, 1, 3):
                r = (x + 4 - d) % 4
                if d:
                    links.wait((last, h, d))
                mine = halves.at[h, r, slots]
                links.start((last, h, 0), mine, mine, tp=1 - c)

        def hand2(h):
            links.wait((last, h, 0))
            for r in range(4):
                for slot in range(4):
                    out[r, 64 * slot : 64 * slot + 64, 128 * h : 128 * h + 128] = halves[h, r, slot]

        return (
            reduce0, reduce1, reduce2, gather0, gather1, gather2, factor, project,
            trace1, hand0, hand1, hand2,
        )

    steps = [iteration(it) for it in range(ITERS)]
    for it, step, j in PLAN:
        steps[it][step](j)

    links.drain()


def subspace_call(owners, keys, basis):
    tokens, width = keys.shape[1], basis.shape[0]
    vm = pltpu.VMEM
    tiles = tokens // TILE
    every = (ITERS, CHUNKS)
    return pl.pallas_call(
        subspace_kernel,
        out_shape=jax.ShapeDtypeStruct((4, 256, 256), B16),
        in_specs=[
            pl.BlockSpec(memory_space=pltpu.SMEM),
            pl.BlockSpec(memory_space=pl.ANY),
            pl.BlockSpec(memory_space=pl.ANY),
        ],
        out_specs=pl.BlockSpec(memory_space=vm),
        scratch_shapes=[
            vm(keys.shape[1:], B16),
            vm((tokens, width), B16),
            vm((width, RANK), B16),
            vm((ITERS, RANK, tokens), B16),
            vm((CHUNKS, B, tokens), F32),
            vm((CHUNKS, B, tokens), F32),
            vm(every + (B, tokens), F32),
            vm(every + (B, tokens), F32),
            vm(every + (B, WIDE), B16),
            vm(every + (B, WIDE), B16),
            vm(every + (B, WIDE), B16),
            vm((CHUNKS, B, WIDE), F32),
            vm(every + (B, WIDE), B16),
            vm(every + (B, WIDE), B16),
            vm(every + (B, WIDE), B16),
            vm(every + (B, WIDE), B16),
            vm(every + (ZS - 1, 16, 256), B16),
            vm(every + (YS, B, WIDE), B16),
            vm((ITERS, 8, 128), F32),
            vm((ITERS, 2 * YS, 8, 128), F32),
            vm((ITERS, 8, 128), F32),
            vm(every + (B, RANK), F32),
            vm(every + (B, RANK), F32),
            vm((RANK, RANK), F32),
            vm((2, 16, 64, 128), B16),
            vm((2, 3, 2, 64, 128), B16),
            vm((2, 4, 4, 64, 128), B16),
            vm((8192, 128), F32),
            pltpu.SemaphoreType.DMA((tiles + 1,)),
            pltpu.SemaphoreType.DMA((2 + ITERS,)),
            pltpu.SemaphoreType.DMA((EVENTS,)),
        ],
        compiler_params=pltpu.CompilerParams(
            collective_id=0, has_side_effects=True, vmem_limit_bytes=VMEM
        ),
        name="subspace",
    )(owners, keys, basis)


def body(keys, start_basis, owner_map):
    basis = start_basis.reshape(-1, start_basis.shape[-1])
    handed = subspace_call(owner_map.reshape(-1), keys, basis)
    return handed[None, None]


def solution(mesh):
    placed = (
        P("req", "seq", None, "tp", None),
        P("req", None, "tp", None, None),
        P("req", "seq", None),
    )
    return jax.shard_map(
        body,
        mesh=mesh,
        in_specs=placed,
        out_specs=P("req", "seq", None, None, None),
        check_vma=False,
    )
```
